128 devices in a mesh: lat: 64 (over z, y, x), lon: 2 (over core).
Axes of the slice: x: 4, y: 4, z: 4, core: 2. Of those that a mesh axis runs over, the one named last changes fastest.
Arguments:
- grid_field: bfloat16 [384, 1440, 512], P('lat', 'lon'), may hold values from -6 to 6
- basis_values: bfloat16 [384, 24, 4], P('lat'), may hold values from -3 to 3
- support_lat: int32 [384, 24], P('lat'), may hold values from -1 to 1
- support_lon: int32 [384, 24], P('lat'), may hold values from -12 to 12
- lon_reach: int32 [384], P('lat'), may hold values from 1 to 12, as said below
- mix_weights: bfloat16 [4, 512, 512], replicated, may hold values from -0.125 to 0.125
Outputs:
- spectra: bfloat16 [2, 640, 384, 512], P(None, 'lat', None, 'lon')
The draws below stay inside these ranges and needn't reach their ends.
Inputs may be any that keep to these rules, and one draw needn't show every extreme that they name: `lon_reach`: roughly larger toward the window's first and last rows, and equal to 12 in both of those rows.
All inputs are finite; a program needn't handle non-finite values.
Results may differ from the reference program's by a relative error of at most 0.0063.
Values may be sent and summed in bfloat16 or wider, within the bound.
No kernel may reach another device: no remote copies, remote signals or barrier semaphores. Data moves between devices by JAX's collectives and lax.ppermute only.
A program may use at most 192 MiB of HBM per device.

```python
import jax
import jax.numpy as jnp
from jax import lax

C = 512
NLON = 1440
MMAX = 640
K = 4
NSUP = 24
RLAT = 1
HMAX = 12
NLAT = 384


def draw_lon_reach(key, part):
    key = jax.random.fold_in(key, 7)
    row_ids = jnp.arange(NLAT, dtype=jnp.int32)
    pole_dist = jnp.minimum(row_ids, NLAT - 1 - row_ids)
    base_reach = jnp.maximum(1, HMAX - pole_dist * 2 * HMAX // NLAT)
    jitter = jax.random.randint(key, (NLAT,), -1, 2, dtype=jnp.int32)
    reach_rows = jnp.clip(base_reach + jitter, 1, HMAX)
    reach_rows = jnp.where(pole_dist == 0, HMAX, reach_rows)
    return reach_rows.astype(jnp.int32)


def with_ends(drawn, key, least, top_value):
    longest = drawn.shape.index(max(drawn.shape))
    spots = []
    for shift in (0, 1):
        where = [jax.random.randint(jax.random.fold_in(key, axis), (), 0, length) for axis, length in enumerate(drawn.shape)]
        where[longest] = (where[longest] + shift) % drawn.shape[longest]
        spots.append(tuple(where))
    return drawn.at[spots[0]].set(least).at[spots[1]].set(top_value)


def level_of(own_key, shape, cuts, smallest, top_value):
    def one(dim, shards_of):
        draws = jax.random.uniform(jax.random.fold_in(jax.random.fold_in(own_key, 6), dim), (shards_of,), jnp.float32, smallest / len(cuts), top_value / len(cuts))
        return jnp.repeat(jnp.exp(draws), shape[dim] // shards_of).reshape((-1,) + (1,) * (len(shape) - dim - 1))

    loudness = one(*cuts[0])
    for cut in cuts[1:]:
        loudness = loudness * one(*cut)
    return loudness


def bell_draw(stream_key, dims, scale, most, shards=(), held_as=jnp.bfloat16):
    values = jax.random.normal(stream_key, dims, jnp.float32) * scale
    if len(shards) > 0:
        values = level_of(stream_key, dims, shards, -0.22, 0.18) * values
    return jnp.clip(values, min=-most, max=most).astype(held_as)


def setup_inputs(seed: int = 0) -> dict:
    splits = jax.random.split(jax.random.key(seed), 7)
    grid_field = bell_draw(splits[0], (NLAT, NLON, C), 1.0, 6.0, ((0, 64), (1, 2)))
    basis_values = bell_draw(splits[1], (NLAT, NSUP, K), 0.2, 3.0, ((0, 64),))
    support_lat = with_ends(jax.random.randint(splits[2], (NLAT, NSUP), 0 - RLAT, RLAT + 1), jax.random.fold_in(splits[2], 1), 0 - RLAT, RLAT).astype(jnp.int32)
    support_lon = with_ends(jax.random.randint(splits[3], (NLAT, NSUP), 0 - HMAX, HMAX + 1), jax.random.fold_in(splits[3], 1), 0 - HMAX, HMAX).astype(jnp.int32)
    lon_reach = draw_lon_reach(jax.random.fold_in(splits[6], 71), 0)
    mix_weights = bell_draw(splits[5], (K, C, C), (K * C) ** -0.5, 0.125)
    return {"grid_field": grid_field, "basis_values": basis_values, "support_lat": support_lat, "support_lon": support_lon, "lon_reach": lon_reach, "mix_weights": mix_weights}


def dft_table(length_lon, mode_count):
    col_ids = jnp.arange(length_lon, dtype=jnp.int32)
    mode_ids = jnp.arange(mode_count, dtype=jnp.int32)
    product = col_ids[:, None] * mode_ids[None, :] % length_lon
    angles = product.astype(jnp.float32) * (2.0 * jnp.pi / length_lon)
    factor = 1.0 / jnp.sqrt(jnp.float32(length_lon))
    return jnp.stack([jnp.cos(angles) * factor, -jnp.sin(angles) * factor], axis=1).astype(jnp.bfloat16)

def reference(grid_field, basis_values, support_lat, support_lon, lon_reach, mix_weights):
    padded = jnp.pad(grid_field, ((RLAT, RLAT), (0, 0), (0, 0)))
    lon_shift = jnp.clip(support_lon, -lon_reach[:, None], lon_reach[:, None]).astype(jnp.int32)
    col_base = jnp.arange(NLON, dtype=jnp.int32)
    twiddle = dft_table(NLON, MMAX).astype(jnp.float32)
    flat_weights = mix_weights.reshape(K * C, C)

    def one_row(row_item):
        row_index, lat_step, lon_step, basis_row = row_item
        src_rows = jnp.take(padded, (row_index + RLAT + lat_step).astype(jnp.int32), axis=0)
        col_index = ((col_base[None, :] + lon_step[:, None]) % NLON).astype(jnp.int32)
        picked = jnp.take_along_axis(src_rows, col_index[:, :, None], axis=1)
        aggregated = jnp.einsum('sjc,sk->jkc', picked.astype(jnp.float32), basis_row.astype(jnp.float32)).astype(jnp.bfloat16)
        convolved = jnp.dot(aggregated.reshape(NLON, K * C), flat_weights, preferred_element_type=jnp.float32)
        activated = jax.nn.gelu(convolved, approximate=False).astype(jnp.bfloat16)
        coeffs = jnp.einsum('jc,jtm->tmc', activated.astype(jnp.float32), twiddle)
        return coeffs.astype(jnp.bfloat16)
    rows_out = lax.map(one_row, (jnp.arange(NLAT, dtype=jnp.int32), support_lat, lon_shift, basis_values))
    return jnp.transpose(rows_out, (1, 2, 0, 3))
```

```python
import functools

import jax
import jax.numpy as jnp
import ml_dtypes
import numpy as np
from jax import lax
from jax.experimental import pallas as pl
from jax.experimental.pallas import tpu as pltpu
from jax.sharding import PartitionSpec as P

MMAX = 640
K = 4
RLAT = 1
HMAX = 12
EDGE = 16
COLS = 48
SPAN = COLS + 2 * EDGE
DEPTH = 256
VMEM = 60 * 1024 * 1024


def exact_gelu(x):
    return 0.5 * x * (1.0 + lax.erf(x * 0.7071067811865476))


def conv_kernel(row_step, sources, table_rows, table_ref, own_ref, mix_hbm, *refs):
    ins, (keep_ref, send_ref, ext, agg, band, mix_ref, sems, mix_sem) = refs[:-8], refs[-8:]
    step = pl.program_id(0)
    support = table_ref.shape[1] // (K + 1)
    lon_cols = keep_ref.shape[1]
    channels = ext.shape[2]
    half = channels // 2
    ext_rows = ext.shape[0]
    steps = (ext_rows - 3) // row_step + 1
    mix_copy = pltpu.make_async_copy(mix_hbm, mix_ref, mix_sem)

    def copies(row):
        pieces = []
        for n, (ref, i, start, size, at) in enumerate(sources[row]):
            pieces.append(
                pltpu.make_async_copy(
                    ins[ref].at[i, pl.ds(start, size)], ext.at[row, pl.ds(at, size)], sems.at[row, n]
                )
            )
        return pieces

    def wait_rows(first, last):
        for row in range(first, last):
            for copy in copies(row):
                copy.wait()

    @pl.when(step == 0)
    def _():
        for row in range(ext_rows):
            for copy in copies(row):
                copy.start()
            if row == 2:
                mix_copy.start()
        wait_rows(0, 3)

    for later in range(1, steps):
        @pl.when(step == later)
        def _(later=later):
            wait_rows(3 + row_step * (later - 1), 3 + row_step * later)

    base = step * row_step
    here = table_rows[0] + step * table_rows[1]

    lanes = lax.broadcasted_iota(jnp.int32, (8, DEPTH), 1).astype(jnp.float32)
    filters = [jnp.zeros((8, DEPTH), jnp.float32) for _ in range(K)]
    for s in range(support):
        hit = lanes == table_ref[here, s]
        for k in range(K):
            filters[k] = filters[k] + jnp.where(hit, table_ref[here, support + s * K + k], 0.0)
    for k in range(K):
        for q in range(0, COLS, 16):
            pair = [
                pltpu.roll(filters[k], q + e, 1, stride=1, stride_axis=0) for e in (0, 8)
            ]
            band[pl.ds(k * COLS + q, 16), :] = jnp.concatenate(pair, axis=0).astype(jnp.bfloat16)

    for start in range(0, lon_cols, COLS):
        window = jnp.concatenate(
            [ext[base + r, pl.ds(start, SPAN), :] for r in range(3)]
            + [ext[base, pl.ds(start, DEPTH - 3 * SPAN), :]],
            axis=0,
        )
        got = jnp.dot(band[...], window, preferred_element_type=jnp.float32).astype(jnp.bfloat16)
        for k in range(K):
            agg[pl.ds(start, COLS), pl.ds(k * channels, channels)] = got[k * COLS : (k + 1) * COLS]

    @pl.when(step == 0)
    def _():
        mix_copy.wait()

    own = own_ref[0]
    for out, part in ((send_ref, 1 - own), (keep_ref, own)):
        weights = mix_ref[:, pl.ds(pl.multiple_of(part * half, half), half)]
        conv = jnp.dot(agg[...], weights, preferred_element_type=jnp.float32)
        out[0] = exact_gelu(conv).astype(out.dtype)


def convolve(row_step, steps, sources, table_rows, table, own, mix, arrays):
    lon_cols, channels = arrays[0].shape[1:]
    smem = pl.BlockSpec(memory_space=pltpu.SMEM)
    hbm = pl.BlockSpec(memory_space=pl.ANY)
    out = jax.ShapeDtypeStruct((steps, lon_cols, channels // 2), jnp.bfloat16)
    out_spec = pl.BlockSpec((1, lon_cols, channels // 2), lambda i: (i, 0, 0))
    ext_rows = len(sources)
    return pl.pallas_call(
        functools.partial(conv_kernel, row_step, sources, table_rows),
        grid=(steps,),
        in_specs=[smem, smem, hbm] + [hbm] * len(arrays),
        out_specs=[out_spec, out_spec],
        out_shape=[out, out],
        scratch_shapes=[
            pltpu.VMEM((ext_rows, lon_cols + 2 * EDGE, channels), jnp.bfloat16),
            pltpu.VMEM((lon_cols, K * channels), jnp.bfloat16),
            pltpu.VMEM((K * COLS, DEPTH), jnp.bfloat16),
            pltpu.VMEM(mix.shape, jnp.bfloat16),
            pltpu.SemaphoreType.DMA((ext_rows, 3)),
            pltpu.SemaphoreType.DMA,
        ],
        compiler_params=pltpu.CompilerParams(
            dimension_semantics=("arbitrary",), vmem_limit_bytes=VMEM
        ),
        cost_estimate=pl.CostEstimate(
            flops=2 * steps * lon_cols * channels * (K * channels + 4 * 256),
            bytes_accessed=2 * (ext_rows + steps) * lon_cols * channels + 2 * mix.size,
            transcendentals=0,
        ),
        name="convolve",
    )(table, own, mix, *arrays)


def twiddles(total_lon, groups):
    half = total_lon // 2
    per = MMAX // groups
    cols = np.arange(half, dtype=np.int64)
    tables = []
    for parity in (0, 1):
        modes = (np.arange(groups)[:, None] * per + np.arange(per // 2)[None, :] * 2 + parity)
        turn = (modes[:, :, None] * cols) % total_lon
        angles = turn.astype(np.float32) * np.float32(2.0 * np.pi / total_lon)
        scale = np.float32(1.0) / np.sqrt(np.float32(total_lon))
        both = np.stack([np.cos(angles) * scale, -np.sin(angles) * scale], axis=1)
        table = np.zeros((MMAX, -(-half // 256) * 256), np.float32)
        table[:, :half] = both.reshape(MMAX, half)
        tables.append(table.astype(ml_dtypes.bfloat16))
    return tables


def zonal_kernel(lats, groups, sign_ref, even_hbm, odd_hbm, ka, ra, kb, rb, out_hbm, *scratch):
    even_ref, odd_ref, keep, recv, lo, hi, out, sems, table_sems, out_sems = scratch
    rows, half, width = keep.shape
    rows_a = ka.shape[0]
    tables = (
        pltpu.make_async_copy(even_hbm, even_ref, table_sems.at[0]),
        pltpu.make_async_copy(odd_hbm, odd_ref, table_sems.at[1]),
    )
    copies = []
    for i in range(rows):
        sides = ((ka, ra), i) if i < rows_a else ((kb, rb), i - rows_a)
        copies.append(
            [
                pltpu.make_async_copy(ref.at[sides[1]], held.at[i], sems.at[i, n])
                for n, (ref, held) in enumerate(zip(sides[0], (keep, recv)))
            ]
        )
    for i in range(rows):
        for copy in copies[i]:
            copy.start()
        if i < 2:
            tables[i].start()

    pad = jnp.zeros((even_ref.shape[1] - half, 2 * width), jnp.bfloat16)
    for i in range(0, rows, 2):
        for copy in copies[i] + copies[i + 1]:
            copy.wait()
        x, y = (
            jnp.concatenate([held[i], held[i + 1]], axis=1).astype(jnp.float32)
            for held in (keep, recv)
        )
        for parity, table, value in ((0, even_ref, x + y), (1, odd_ref, (x - y) * sign_ref[0])):
            if i == 0:
                tables[parity].wait()
            folded = jnp.concatenate([value.astype(jnp.bfloat16), pad], axis=0)
            got = jnp.dot(table[...], folded, preferred_element_type=jnp.float32)
            for e in (0, 1):
                where = pl.ds(parity * rows + lats[i + e], MMAX, stride=2 * rows)
                lo[where, :] = got[:, e * width : e * width + 128]
                hi[where, :] = got[:, e * width + 128 : (e + 1) * width]

    size = out.shape[1]
    batch = groups // out_sems.shape[0]

    def send(b):
        at = pl.ds(b * batch, batch)
        return pltpu.make_async_copy(out.at[at], out_hbm.at[at], out_sems.at[b])

    for b in range(out_sems.shape[0]):
        for g in range(b * batch, (b + 1) * batch):
            at = pl.ds(g * size, size)
            out[g, :, pl.ds(0, 128)] = lo[at, :].astype(out.dtype)
            out[g, :, pl.ds(128, 128)] = hi[at, :].astype(out.dtype)
        send(b).start()
    for b in range(out_sems.shape[0]):
        send(b).wait()


def zonal(sign, keep_a, recv_a, keep_b, recv_b, lats, groups):
    rows_a, half, width = keep_a.shape
    rows = rows_a + keep_b.shape[0]
    even, odd = (jnp.asarray(t) for t in twiddles(2 * half, groups))
    hbm = pl.BlockSpec(memory_space=pl.ANY)
    block = (groups, 2 * MMAX // groups * rows, width)
    return pl.pallas_call(
        functools.partial(zonal_kernel, lats, groups),
        in_specs=[pl.BlockSpec(memory_space=pltpu.SMEM)] + [hbm] * 6,
        out_specs=hbm,
        out_shape=jax.ShapeDtypeStruct(block, jnp.bfloat16),
        scratch_shapes=[
            pltpu.VMEM(even.shape, jnp.bfloat16),
            pltpu.VMEM(odd.shape, jnp.bfloat16),
            pltpu.VMEM((rows, half, width), jnp.bfloat16),
            pltpu.VMEM((rows, half, width), jnp.bfloat16),
            pltpu.VMEM((2 * MMAX * rows, 128), jnp.float32),
            pltpu.VMEM((2 * MMAX * rows, 128), jnp.float32),
            pltpu.VMEM(block, jnp.bfloat16),
            pltpu.SemaphoreType.DMA((rows, 2)),
            pltpu.SemaphoreType.DMA((2,)),
            pltpu.SemaphoreType.DMA((8,)),
        ],
        compiler_params=pltpu.CompilerParams(vmem_limit_bytes=VMEM),
        cost_estimate=pl.CostEstimate(
            flops=4 * rows * MMAX * even.shape[1] * width,
            bytes_accessed=2 * (2 * rows * half * width + 2 * even.size + 2 * MMAX * rows * width),
            transcendentals=0,
        ),
        name="zonal",
    )(sign, even, odd, keep_a, recv_a, keep_b, recv_b)


def gather_kernel(rows, in_ref, out_ref, wide, laid):
    sources, size, width = in_ref.shape
    modes = size // rows
    for c in range(0, width, 128):
        at = pl.ds(c, 128)
        for g in range(sources):
            wide[pl.ds(g * size, size), :] = in_ref[g, :, at].astype(jnp.float32)
        for m in range(modes):
            for i in range(rows):
                piece = wide[pl.ds(m * rows + i, sources, stride=size), :]
                laid[pl.ds(m * sources * rows + i, sources, stride=rows), :] = piece
        for m in range(modes):
            out_ref[m, :, at] = laid[pl.ds(m * sources * rows, sources * rows), :].astype(out_ref.dtype)


def gather(moved, rows):
    bands, size, width = moved.shape
    batch = 8
    modes = size // rows
    return pl.pallas_call(
        functools.partial(gather_kernel, rows),
        grid=(bands // batch,),
        in_specs=[pl.BlockSpec((batch, size, width), lambda g: (g, 0, 0))],
        out_specs=pl.BlockSpec((modes, batch * rows, width), lambda g: (0, g, 0)),
        out_shape=jax.ShapeDtypeStruct((modes, bands * rows, width), moved.dtype),
        scratch_shapes=[
            pltpu.VMEM((batch * size, 128), jnp.float32),
            pltpu.VMEM((batch * size, 128), jnp.float32),
        ],
        compiler_params=pltpu.CompilerParams(
            dimension_semantics=("arbitrary",), vmem_limit_bytes=VMEM
        ),
        name="gather",
    )(moved)


def body(grid_field, basis_values, support_lat, support_lon, lon_reach, mix_weights):
    lat_rows, lon_cols, channels = grid_field.shape
    bands = lax.axis_size("lat")
    own = lax.axis_index("lon")
    swap = [(0, 1), (1, 0)]
    ahead = [(i, i + 1) for i in range(bands - 1)]
    back = [(b, a) for a, b in ahead]
    last = lat_rows - 1

    edge = jnp.concatenate([grid_field[:, :EDGE], grid_field[:, lon_cols - EDGE :]], axis=1)
    edges = lax.ppermute(edge, "lon", swap)

    def wide_row(row):
        return jnp.concatenate(
            [edges[row, EDGE:], grid_field[row], edges[row, :EDGE]], axis=0
        )[None]

    low = lax.ppermute(wide_row(last), "lat", ahead)
    high = lax.ppermute(wide_row(0), "lat", back)

    shift = jnp.clip(support_lon, -lon_reach[:, None], lon_reach[:, None])
    index = ((support_lat + RLAT) * SPAN + EDGE + shift).astype(jnp.float32)
    basis = basis_values.astype(jnp.float32).reshape(lat_rows, -1)
    table = jnp.concatenate([index, basis], axis=1)
    mix = mix_weights.reshape(K * channels, channels)
    own_1 = own.astype(jnp.int32).reshape(1)

    def own_row(row):
        return (
            (0, row, 0, lon_cols, EDGE),
            (1, row, EDGE, EDGE, 0),
            (1, row, 0, EDGE, EDGE + lon_cols),
        )

    def beside(ref):
        return ((ref, 0, 0, lon_cols + 2 * EDGE, 0),)

    keep_a, send_a = convolve(
        1, lat_rows - 2, [own_row(r) for r in range(lat_rows)], (1, 1), table, own_1, mix,
        [grid_field, edges],
    )
    recv_a = lax.ppermute(send_a, "lon", swap)
    outer = [beside(2), own_row(0), own_row(1), own_row(last - 1), own_row(last), beside(3)]
    keep_b, send_b = convolve(
        3, 2, outer, (0, last), table, own_1, mix, [grid_field, edges, low, high]
    )
    recv_b = lax.ppermute(send_b, "lon", swap)
    sign = (1 - 2 * own).astype(jnp.float32).reshape(1)
    lats = list(range(1, last)) + [0, last]
    packed = zonal(sign, keep_a, recv_a, keep_b, recv_b, lats, bands)
    moved = lax.all_to_all(packed, "lat", 0, 0, tiled=True)
    out = gather(moved, lat_rows)
    return out.reshape(2, MMAX // bands, bands * lat_rows, channels // 2)


def solution(mesh):
    return jax.shard_map(
        body,
        mesh=mesh,
        in_specs=(
            P("lat", "lon", None),
            P("lat", None, None),
            P("lat", None),
            P("lat", None),
            P("lat"),
            P(),
        ),
        out_specs=P(None, "lat", None, "lon"),
        check_vma=False,
    )
```

```python
import functools

import jax
import jax.numpy as jnp
import ml_dtypes
import numpy as np
from jax import lax
from jax.experimental import pallas as pl
from jax.experimental.pallas import tpu as pltpu
from jax.sharding import PartitionSpec as P

MMAX = 640
K = 4
RLAT = 1
HMAX = 12
EDGE = 16
COLS = 48
SPAN = COLS + 2 * EDGE
DEPTH = 256
PITCH = 49
VMEM = 62 * 1024 * 1024


def exact_gelu(x):
    return 0.5 * x * (1.0 + lax.erf(x * 0.7071067811865476))


def row_kernel(joins, at, outer, lat, table_ref, own_ref, mix_hbm, even_hbm, odd_hbm, *refs):
    n_in = 2 + 2 * outer + joins
    ins, out_hbm, scratch = refs[:n_in], refs[n_in], refs[n_in + 1 :]
    ext, agg, band, added, taken, left, out, mix_ref, even_ref, odd_ref = scratch[:10]
    row_sems, own_sems, out_sems = scratch[10:]
    own = own_ref[0]
    support = table_ref.shape[1] // (K + 1)
    half_lon = ins[0].shape[1]
    total_lon = 2 * half_lon
    channels = ext.shape[2]
    rows = ext.shape[0] - 2
    groups = out.shape[0]

    def columns(side):
        return pl.ds(pl.multiple_of(EDGE + side * half_lon, 16), half_lon)

    def sides(n, mine, other, at_row):
        return (
            pltpu.make_async_copy(mine, ext.at[at_row, columns(own)], row_sems.at[n, 0]),
            pltpu.make_async_copy(other, ext.at[at_row, columns(1 - own)], row_sems.at[n, 1]),
        )

    field, swapped = ins[0], ins[1]
    if outer:
        copies = [
            sides(k, field.at[4 * own + k], swapped.at[4 * own + k], 1 - own + k) for k in (0, 1)
        ]
        copies.append(sides(2, ins[2].at[0], ins[3].at[0], 2 * own))
    else:
        copies = [sides(k, field.at[2 * own + k], swapped.at[2 * own + k], k) for k in range(rows + 2)]
    mix_copy = pltpu.make_async_copy(mix_hbm, mix_ref, own_sems.at[0])
    table_copies = (
        pltpu.make_async_copy(even_hbm, even_ref, own_sems.at[1]),
        pltpu.make_async_copy(odd_hbm, odd_ref, own_sems.at[2]),
    )
    for pair in copies[:3]:
        for copy in pair:
            copy.start()

    pad = added.shape[0] - half_lon
    added[pl.ds(half_lon, pad), :] = jnp.zeros((pad, channels), added.dtype)
    taken[pl.ds(half_lon, pad), :] = jnp.zeros((pad, channels), added.dtype)
    lanes = lax.broadcasted_iota(jnp.int32, (8, DEPTH), 1).astype(jnp.float32)

    sends = []

    def send(side, start, size, n):
        copy = pltpu.make_async_copy(
            out.at[:, side, pl.ds(start, size)],
            out_hbm.at[:, side, pl.ds(at + start, size)],
            out_sems.at[n, side],
        )
        copy.start()
        sends.append(copy)

    for step in range(rows):
        first = 0 if step == 0 else step + 2
        for pair in copies[first : step + 3]:
            for copy in pair:
                copy.wait()
        for e in range(first, step + 3):
            ext[e, pl.ds(0, EDGE), :] = ext[e, pl.ds(total_lon, EDGE), :]
            ext[e, pl.ds(EDGE + total_lon, EDGE), :] = ext[e, pl.ds(EDGE, EDGE), :]
        if step == 0:
            mix_copy.start()
            for pair in (*copies[3:], table_copies):
                for copy in pair:
                    copy.start()

        here = lat[0] + lat[1] * own + step
        filters = [jnp.zeros((8, DEPTH), jnp.float32) for _ in range(K)]
        for s in range(support):
            hit = lanes == table_ref[here, s]
            for k in range(K):
                filters[k] = filters[k] + jnp.where(hit, table_ref[here, support + s * K + k], 0.0)
        for k in range(K):
            for q in range(0, COLS, 16):
                pair = [
                    pltpu.roll(filters[k], q + e, 1, stride=1, stride_axis=0) for e in (0, 8)
                ]
                band[pl.ds(k * COLS + q, 16), :] = jnp.concatenate(pair, axis=0).astype(band.dtype)

        for start in range(0, total_lon, COLS):
            window = jnp.concatenate(
                [ext[step + r, pl.ds(start, SPAN), :] for r in range(3)]
                + [ext[step, pl.ds(start, DEPTH - 3 * SPAN), :]],
                axis=0,
            )
            got = jnp.dot(band[...], window, preferred_element_type=jnp.float32).astype(agg.dtype)
            for k in range(K):
                agg[pl.ds(start, COLS), pl.ds(k * channels, channels)] = got[k * COLS : (k + 1) * COLS]

        if step == 0:
            mix_copy.wait()
        width = channels // 2
        for n in range(0, channels, width):
            at_n = pl.ds(n, width)
            near, far = (
                exact_gelu(
                    jnp.dot(
                        agg[pl.ds(j, half_lon), :], mix_ref[:, at_n], preferred_element_type=jnp.float32
                    )
                )
                for j in (0, half_lon)
            )
            added[pl.ds(0, half_lon), at_n] = (near + far).astype(added.dtype)
            taken[pl.ds(0, half_lon), at_n] = (near - far).astype(taken.dtype)

        if step == 0:
            for copy in table_copies:
                copy.wait()
        for side in (0, 1):
            at_n = pl.ds(side * width, width)
            even = jnp.dot(even_ref[...], added[:, at_n], preferred_element_type=jnp.float32)
            odd = jnp.dot(odd_ref[...], taken[:, at_n], preferred_element_type=jnp.float32)
            main = jnp.concatenate(
                [got[: groups * 8].reshape(groups, 8, width) for got in (even, odd)], axis=1
            ).astype(out.dtype)
            for h in (0, 1):
                c = 2 * step + h
                out[:, side, pl.ds(16 * c, 16), :] = main[:, :, h * 128 : (h + 1) * 128]
                for parity, got in ((0, even), (1, odd)):
                    for e in (0, 1):
                        where = pl.ds(4 * c + 2 * e + parity, groups, stride=8 * rows)
                        rest = got[groups * (8 + e) : groups * (9 + e), h * 128 : (h + 1) * 128]
                        left[side, where, :] = rest

            send(side, 32 * step, 32, step)

    size = 8 * rows
    for side in (0, 1):
        rest = left[side].reshape(groups, size, 128)
        out[:, side, pl.ds(32 * rows, size), :] = rest.astype(out.dtype)
        send(side, 32 * rows, size, rows)
    for copy in sends:
        copy.wait()


def circle_rows(rows, at, lat, table, own, mix, even, odd, arrays, joined=None):
    _, half_lon, channels = arrays[0].shape
    groups = MMAX // 10
    smem = pl.BlockSpec(memory_space=pltpu.SMEM)
    hbm = pl.BlockSpec(memory_space=pl.ANY)
    given = list(arrays) + ([] if joined is None else [joined])
    wire = jax.ShapeDtypeStruct((groups, 2, 120, 128), jnp.bfloat16)
    return pl.pallas_call(
        functools.partial(row_kernel, int(joined is not None), at, int(len(arrays) > 2), lat),
        in_specs=[smem, smem] + [hbm] * (3 + len(given)),
        out_specs=hbm,
        out_shape=wire,
        input_output_aliases={} if joined is None else {4 + len(given): 0},
        scratch_shapes=[
            pltpu.VMEM((rows + 2, 2 * half_lon + 2 * EDGE, channels), jnp.bfloat16),
            pltpu.VMEM((2 * half_lon, K * channels), jnp.bfloat16),
            pltpu.VMEM((K * COLS, DEPTH), jnp.bfloat16),
            pltpu.VMEM((even.shape[1], channels), jnp.bfloat16),
            pltpu.VMEM((even.shape[1], channels), jnp.bfloat16),
            pltpu.VMEM((2, groups * 8 * rows, 128), jnp.float32),
            pltpu.VMEM((groups, 2, 40 * rows, 128), jnp.bfloat16),
            pltpu.VMEM(mix.shape, jnp.bfloat16),
            pltpu.VMEM(even.shape, jnp.bfloat16),
            pltpu.VMEM(odd.shape, jnp.bfloat16),
            pltpu.SemaphoreType.DMA((rows + 2, 2)),
            pltpu.SemaphoreType.DMA((3,)),
            pltpu.SemaphoreType.DMA((rows + 1, 2)),
        ],
        compiler_params=pltpu.CompilerParams(vmem_limit_bytes=VMEM),
        cost_estimate=pl.CostEstimate(
            flops=rows * (4 * half_lon * channels * (K * channels + 1024) + 4 * MMAX * half_lon * channels),
            bytes_accessed=4 * (rows + 2) * half_lon * channels + 2 * mix.size + 4 * even.size,
            transcendentals=0,
        ),
        name="circle_rows",
    )(table, own, mix, even, odd, *given)


def twiddles(total_lon, groups):
    half = total_lon // 2
    per = MMAX // groups
    cols = np.arange(half, dtype=np.int64)
    g = np.arange(groups)
    tables = []
    for parity in (0, 1):
        pairs = [(n, q) for n in g for q in range(8)] + [(n, q) for q in (8, 9) for n in g]
        group, place = np.array(pairs).T
        place = 2 * place + parity
        part, mode = place // per, group * per + place % per
        turn = (mode[:, None] * cols) % total_lon
        angles = turn.astype(np.float32) * np.float32(2.0 * np.pi / total_lon)
        scale = np.float32(1.0) / np.sqrt(np.float32(total_lon))
        table = np.zeros((MMAX, -(-half // 256) * 256), np.float32)
        table[:, :half] = np.where(part[:, None] == 0, np.cos(angles), -np.sin(angles)) * scale
        tables.append(table.astype(ml_dtypes.bfloat16))
    return tables


def gather_kernel(in_hbm, out_hbm, held, laid_0, laid_1, out, in_sems, out_sems):
    batches, sources, _, _ = held.shape
    modes, rows = out.shape[1:3]
    per = rows // sources
    laid = (laid_0, laid_1)

    def fetch(b):
        return pltpu.make_async_copy(in_hbm.at[pl.ds(b * sources, sources)], held.at[b], in_sems.at[b])

    def place(b):
        return pltpu.make_async_copy(out.at[b], out_hbm.at[:, pl.ds(b * rows, rows)], out_sems.at[b])

    def start(b, carry):
        fetch(b).start()
        return carry

    lax.fori_loop(0, batches, start, 0)

    def one(b, carry):
        fetch(b).wait()
        for g in range(sources):
            block = held[b, g].astype(jnp.float32)
            for step in range(per):
                lat = step if g % 2 else (step + 1) % per
                for h in (0, 1):
                    c = 2 * step + h
                    main, rest = (16 * c, 64 + 4 * c) if step < 2 else (80 + 16 * h, 112 + 4 * h)
                    to = g * per + lat
                    laid[h][pl.ds(to, 8, stride=PITCH), :] = block[main : main + 8]
                    laid[h][pl.ds(8 * PITCH + to, 8, stride=PITCH), :] = block[main + 8 : main + 16]
                    laid[h][pl.ds(16 * PITCH + to, 4, stride=PITCH), :] = block[rest : rest + 4]
        for m in range(modes):
            slot = 8 * (m % 2) + m // 2 if m < 16 else m
            for h in (0, 1):
                piece = laid[h][pl.ds(slot * PITCH, rows), :]
                out[b, m, :, pl.ds(128 * h, 128)] = piece.astype(out.dtype)
        place(b).start()
        return carry

    lax.fori_loop(0, batches, one, 0)

    def end(b, carry):
        place(b).wait()
        return carry

    lax.fori_loop(0, batches, end, 0)


def gather(moved):
    total, size, width = moved.shape
    sources = 16
    batches = total // sources
    modes = size // 6
    hbm = pl.BlockSpec(memory_space=pl.ANY)
    return pl.pallas_call(
        gather_kernel,
        in_specs=[hbm],
        out_specs=hbm,
        out_shape=jax.ShapeDtypeStruct((modes, total * 3, 2 * width), moved.dtype),
        scratch_shapes=[
            pltpu.VMEM((batches, sources, size, width), moved.dtype),
            pltpu.VMEM((modes * PITCH, 128), jnp.float32),
            pltpu.VMEM((modes * PITCH, 128), jnp.float32),
            pltpu.VMEM((batches, modes, sources * 3, 2 * width), moved.dtype),
            pltpu.SemaphoreType.DMA((batches,)),
            pltpu.SemaphoreType.DMA((batches,)),
        ],
        compiler_params=pltpu.CompilerParams(vmem_limit_bytes=VMEM),
        name="gather",
    )(moved)


def body(grid_field, basis_values, support_lat, support_lon, lon_reach, mix_weights):
    lat_rows, half_lon, channels = grid_field.shape
    bands = lax.axis_size("lat")
    own = lax.axis_index("lon").astype(jnp.int32)
    both = ("lat", "lon")
    last = lat_rows - 1

    swapped = lax.ppermute(grid_field, "lon", [(0, 1), (1, 0)])
    up = range(bands - 1)
    same = [(2 * b, 2 * b + 2) for b in up] + [(2 * b + 3, 2 * b + 1) for b in up]
    cross = [(2 * b + 1, 2 * b + 2) for b in up] + [(2 * b + 2, 2 * b + 1) for b in up]
    ends = (grid_field[last:], grid_field[:1])
    beside_1 = lax.ppermute(jnp.where(own == 0, *ends), both, same)
    beside_2 = lax.ppermute(jnp.where(own == 1, *ends), both, cross)

    shift = jnp.clip(support_lon, -lon_reach[:, None], lon_reach[:, None])
    index = ((support_lat + RLAT) * SPAN + EDGE + shift).astype(jnp.float32)
    basis = basis_values.astype(jnp.float32).reshape(lat_rows, -1)
    table = jnp.concatenate([index, basis], axis=1)
    mix = mix_weights.reshape(K * channels, channels)
    even, odd = (jnp.asarray(t) for t in twiddles(2 * half_lon, bands))
    own_1 = own.reshape(1)

    inner = circle_rows(2, 0, (1, 2), table, own_1, mix, even, odd, [grid_field, swapped])
    packed = circle_rows(
        1, 80, (0, last), table, own_1, mix, even, odd,
        [grid_field, swapped, beside_1, beside_2], inner,
    )
    packed = packed.reshape(2 * bands, packed.shape[2], packed.shape[3])
    moved = lax.all_to_all(packed, both, 0, 0, tiled=True)
    return gather(moved).reshape(2, MMAX // bands, bands * lat_rows, channels // 2)


def solution(mesh):
    return jax.shard_map(
        body,
        mesh=mesh,
        in_specs=(
            P("lat", "lon", None),
            P("lat", None, None),
            P("lat", None),
            P("lat", None),
            P("lat"),
            P(),
        ),
        out_specs=P(None, "lat", None, "lon"),
        check_vma=False,
    )
```

```python
import functools

import jax
import jax.numpy as jnp
import ml_dtypes
import numpy as np
from jax import lax
from jax.experimental import pallas as pl
from jax.experimental.pallas import tpu as pltpu
from jax.sharding import PartitionSpec as P

MMAX = 640
K = 4
RLAT = 1
HMAX = 12
EDGE = 16
COLS = 48
SPAN = COLS + 2 * EDGE
DEPTH = 256
PITCH = 49
VMEM = 62 * 1024 * 1024


def exact_gelu(x):
    return 0.5 * x * (1.0 + lax.erf(x * 0.7071067811865476))


def row_kernel(outer, lat_ref, lon_ref, reach_ref, own_ref, basis_ref, *refs):
    mix_hbm, even_hbm, odd_hbm = refs[:3]
    n_in = 3 + 2 + 2 * outer
    ins, out_hbm, scratch = refs[3:n_in], refs[n_in], refs[n_in + 1 :]
    ext, agg, band, first, added, taken, left, out, mix_ref, even_ref, odd_ref = scratch[:11]
    row_sems, own_sems, out_sems = scratch[11:]
    own = own_ref[0]
    support = lat_ref.shape[1]
    half_lon = ins[0].shape[1]
    total_lon = 2 * half_lon
    channels = ext.shape[2]
    rows = ext.shape[0] - 2
    groups = out.shape[0]

    near_pieces = ((0, 0, half_lon), (1, 0, EDGE), (1, half_lon - EDGE, EDGE))
    pieces = (*near_pieces, (1, EDGE, half_lon - 2 * EDGE))

    def copy_of(n, p, core):
        side, begin, size = pieces[p]
        (ref, row), at_row = sources[n][side != core], sources[n][2]
        to = ext.at[at_row, pl.ds(EDGE + side * half_lon + begin, size)]
        return pltpu.make_async_copy(ref.at[row, pl.ds(begin, size)], to, row_sems.at[n, p])

    def start(n, p):
        for core in (0, 1):
            @pl.when(own == core)
            def _(core=core):
                copy_of(n, p, core).start()

    def wait(n, p):
        copy_of(n, p, 0).wait()

    field, swapped = ins[0], ins[1]
    if outer:
        sources = [((field, 3 * own + n), (swapped, 3 * own + n), 1 - own + n) for n in range(3)]
        sources.append(((ins[2], 0), (ins[3], 0), 3 * own))
        bases = [1 - own + step * (2 * own - 1) for step in range(rows)]
        lats = [4 * own + base for base in bases]
    else:
        sources = [((field, 1 + own + n), (swapped, 1 + own + n), n) for n in range(3)]
        bases, lats = [0], [2 + own]
    mix_copy = pltpu.make_async_copy(mix_hbm, mix_ref, own_sems.at[0])
    table_copies = (
        pltpu.make_async_copy(even_hbm, even_ref, own_sems.at[1]),
        pltpu.make_async_copy(odd_hbm, odd_ref, own_sems.at[2]),
    )
    for n in range(3):
        for p in range(3):
            start(n, p)
    mix_copy.start()
    for n in range(3):
        start(n, 3)
    for copy in table_copies:
        copy.start()
    for n in range(3, rows + 2):
        for p in range(4):
            start(n, p)

    pad = added.shape[0] - half_lon
    added[pl.ds(half_lon, pad), :] = jnp.zeros((pad, channels), added.dtype)
    taken[pl.ds(half_lon, pad), :] = jnp.zeros((pad, channels), added.dtype)
    sends = []

    def send(side, begin, size, n):
        copy = pltpu.make_async_copy(
            out.at[:, side, pl.ds(begin, size)],
            out_hbm.at[:, side, pl.ds(begin, size)],
            out_sems.at[n, side],
        )
        copy.start()
        sends.append(copy)

    lanes = lax.broadcasted_iota(jnp.int32, (support, DEPTH), 1)
    points = lax.broadcasted_iota(jnp.int32, (support, DEPTH), 0)
    width = channels // 2
    rest_size = 8 * rows
    for step in range(rows):
        here, base = lats[step], bases[step]
        reach = reach_ref[here]
        index = jnp.zeros((support, DEPTH), jnp.int32)
        for s in range(support):
            shift = jnp.minimum(jnp.maximum(lon_ref[here, s], -reach), reach)
            lane = (lat_ref[here, s] + RLAT) * SPAN + EDGE + shift
            index = jnp.where(points == s, lane, index)
        hits = jnp.where(lanes == index, 1.0, 0.0).astype(jnp.bfloat16)
        filters = jnp.dot(basis_ref[here], hits, preferred_element_type=jnp.float32)
        for k in range(K):
            same = jnp.broadcast_to(filters[k : k + 1], (8, DEPTH))
            for q in range(0, COLS, 16):
                pair = [pltpu.roll(same, q + e, 1, stride=1, stride_axis=0) for e in (0, 8)]
                band[pl.ds(k * COLS + q, 16), :] = jnp.concatenate(pair, axis=0).astype(band.dtype)

        fresh = range(0, 3) if step == 0 else range(step + 2, step + 3)
        for half in (0, 1):
            for n in fresh:
                for p in (range(3) if half == 0 else (3,)):
                    wait(n, p)
            if half == 0:
                for e in (sources[n][2] for n in fresh):
                    ext[e, pl.ds(0, EDGE), :] = ext[e, pl.ds(total_lon, EDGE), :]
                    ext[e, pl.ds(EDGE + total_lon, EDGE), :] = ext[e, pl.ds(EDGE, EDGE), :]
            for begin in range(half * half_lon, (half + 1) * half_lon, COLS):
                window = jnp.concatenate(
                    [ext[base + r, pl.ds(begin, SPAN), :] for r in range(3)]
                    + [ext[base, pl.ds(begin, DEPTH - 3 * SPAN), :]],
                    axis=0,
                )
                got = jnp.dot(band[...], window, preferred_element_type=jnp.float32).astype(agg.dtype)
                for k in range(K):
                    to = pl.ds(begin - half * half_lon, COLS), pl.ds(k * channels, channels)
                    agg[half, *to] = got[k * COLS : (k + 1) * COLS]
            if step == 0 and half == 0:
                mix_copy.wait()
            for n in range(0, channels, width):
                at_n = pl.ds(n, width)
                active = exact_gelu(
                    jnp.dot(agg[half], mix_ref[:, at_n], preferred_element_type=jnp.float32)
                )
                if half == 0:
                    first[:, at_n] = active
                else:
                    added[pl.ds(0, half_lon), at_n] = (first[:, at_n] + active).astype(added.dtype)
                    taken[pl.ds(0, half_lon), at_n] = (first[:, at_n] - active).astype(taken.dtype)

        if step == 0:
            for copy in table_copies:
                copy.wait()
        for side in (0, 1):
            at_n = pl.ds(side * width, width)
            even = jnp.dot(even_ref[...], added[:, at_n], preferred_element_type=jnp.float32)
            odd = jnp.dot(odd_ref[...], taken[:, at_n], preferred_element_type=jnp.float32)
            main = jnp.concatenate(
                [got[: groups * 8].reshape(groups, 8, width) for got in (even, odd)], axis=1
            ).astype(out.dtype)
            for h in (0, 1):
                c = 2 * step + h
                out[:, side, pl.ds(16 * c, 16), :] = main[:, :, h * 128 : (h + 1) * 128]
                for parity, got in ((0, even), (1, odd)):
                    for e in (0, 1):
                        where = pl.ds(4 * c + 2 * e + parity, groups, stride=rest_size)
                        rest = got[groups * (8 + e) : groups * (9 + e), h * 128 : (h + 1) * 128]
                        left[side, where, :] = rest
            send(side, 32 * step, 32, step)
            if step == rows - 1:
                rest = left[side].reshape(groups, rest_size, 128)
                out[:, side, pl.ds(32 * rows, rest_size), :] = rest.astype(out.dtype)
                send(side, 32 * rows, rest_size, rows)
    for copy in sends:
        copy.wait()


def circle_rows(rows, support, own, basis, mix, even, odd, arrays):
    _, half_lon, channels = arrays[0].shape
    groups = MMAX // 10
    smem = pl.BlockSpec(memory_space=pltpu.SMEM)
    hbm = pl.BlockSpec(memory_space=pl.ANY)
    wire = jax.ShapeDtypeStruct((groups, 2, 40 * rows, 128), jnp.bfloat16)
    return pl.pallas_call(
        functools.partial(row_kernel, int(len(arrays) > 2)),
        in_specs=[smem] * 4 + [pl.BlockSpec(memory_space=pltpu.VMEM)] + [hbm] * (3 + len(arrays)),
        out_specs=hbm,
        out_shape=wire,
        scratch_shapes=[
            pltpu.VMEM((rows + 2, 2 * half_lon + 2 * EDGE, channels), jnp.bfloat16),
            pltpu.VMEM((2, half_lon, K * channels), jnp.bfloat16),
            pltpu.VMEM((K * COLS, DEPTH), jnp.bfloat16),
            pltpu.VMEM((half_lon, channels), jnp.float32),
            pltpu.VMEM((even.shape[1], channels), jnp.bfloat16),
            pltpu.VMEM((even.shape[1], channels), jnp.bfloat16),
            pltpu.VMEM((2, groups * 8 * rows, 128), jnp.float32),
            pltpu.VMEM((groups, 2, 40 * rows, 128), jnp.bfloat16),
            pltpu.VMEM(mix.shape, jnp.bfloat16),
            pltpu.VMEM(even.shape, jnp.bfloat16),
            pltpu.VMEM(odd.shape, jnp.bfloat16),
            pltpu.SemaphoreType.DMA((rows + 2, 4)),
            pltpu.SemaphoreType.DMA((3,)),
            pltpu.SemaphoreType.DMA((rows + 1, 2)),
        ],
        compiler_params=pltpu.CompilerParams(vmem_limit_bytes=VMEM),
        cost_estimate=pl.CostEstimate(
            flops=rows * (4 * half_lon * channels * (K * channels + 1024) + 4 * MMAX * half_lon * channels),
            bytes_accessed=4 * (rows + 2) * half_lon * channels + 2 * mix.size + 4 * even.size,
            transcendentals=0,
        ),
        name="circle_rows",
    )(*support, own, basis, mix, even, odd, *arrays)


def twiddles(total_lon, groups):
    half = total_lon // 2
    per = MMAX // groups
    cols = np.arange(half, dtype=np.int64)
    g = np.arange(groups)
    tables = []
    for parity in (0, 1):
        pairs = [(n, q) for n in g for q in range(8)] + [(n, q) for q in (8, 9) for n in g]
        group, place = np.array(pairs).T
        place = 2 * place + parity
        part, mode = place // per, group * per + place % per
        turn = (mode[:, None] * cols) % total_lon
        angles = turn.astype(np.float32) * np.float32(2.0 * np.pi / total_lon)
        scale = np.float32(1.0) / np.sqrt(np.float32(total_lon))
        table = np.zeros((MMAX, -(-half // 256) * 256), np.float32)
        table[:, :half] = np.where(part[:, None] == 0, np.cos(angles), -np.sin(angles)) * scale
        tables.append(table.astype(ml_dtypes.bfloat16))
    return tables


def gather_kernel(in_1, in_2, out_hbm, held_1, held_2, laid_0, laid_1, out, in_sems, out_sems):
    batches, sources, _, _ = held_1.shape
    modes, rows = out.shape[1:3]
    per = rows // sources
    laid = (laid_0, laid_1)

    def fetch(b, n):
        ref, held = ((in_1, held_1), (in_2, held_2))[n]
        return pltpu.make_async_copy(ref.at[pl.ds(b * sources, sources)], held.at[b], in_sems.at[b, n])

    def place(b):
        return pltpu.make_async_copy(out.at[b], out_hbm.at[:, pl.ds(b * rows, rows)], out_sems.at[b])

    def start(b, carry):
        for n in (0, 1):
            fetch(b, n).start()
        return carry

    lax.fori_loop(0, batches, start, 0)

    def one(b, carry):
        for n in (0, 1):
            fetch(b, n).wait()
        for g in range(sources):
            blocks = [held[b, g].astype(jnp.float32) for held in (held_1, held_2)]
            for step in range(per):
                lat = step if g % 2 else per - 1 - step
                for h in (0, 1):
                    if step == 0:
                        block, main, rest = blocks[0], 16 * h, 32 + 4 * h
                    else:
                        c = 2 * (step - 1) + h
                        block, main, rest = blocks[1], 16 * c, 64 + 4 * c
                    to = g * per + lat
                    laid[h][pl.ds(to, 8, stride=PITCH), :] = block[main : main + 8]
                    laid[h][pl.ds(8 * PITCH + to, 8, stride=PITCH), :] = block[main + 8 : main + 16]
                    laid[h][pl.ds(16 * PITCH + to, 4, stride=PITCH), :] = block[rest : rest + 4]
        for m in range(modes):
            slot = 8 * (m % 2) + m // 2 if m < 16 else m
            for h in (0, 1):
                piece = laid[h][pl.ds(slot * PITCH, rows), :]
                out[b, m, :, pl.ds(128 * h, 128)] = piece.astype(out.dtype)
        place(b).start()
        return carry

    lax.fori_loop(0, batches, one, 0)

    def end(b, carry):
        place(b).wait()
        return carry

    lax.fori_loop(0, batches, end, 0)


def gather(moved_1, moved_2):
    total, size, width = moved_1.shape
    sources = 16
    batches = total // sources
    modes = size // 2
    hbm = pl.BlockSpec(memory_space=pl.ANY)
    return pl.pallas_call(
        gather_kernel,
        in_specs=[hbm, hbm],
        out_specs=hbm,
        out_shape=jax.ShapeDtypeStruct((modes, total * 3, 2 * width), moved_1.dtype),
        scratch_shapes=[
            pltpu.VMEM((batches, sources, size, width), moved_1.dtype),
            pltpu.VMEM((batches, sources, 2 * size, width), moved_1.dtype),
            pltpu.VMEM((modes * PITCH, 128), jnp.float32),
            pltpu.VMEM((modes * PITCH, 128), jnp.float32),
            pltpu.VMEM((batches, modes, sources * 3, 2 * width), moved_1.dtype),
            pltpu.SemaphoreType.DMA((batches, 2)),
            pltpu.SemaphoreType.DMA((batches,)),
        ],
        compiler_params=pltpu.CompilerParams(vmem_limit_bytes=VMEM),
        name="gather",
    )(moved_1, moved_2)


def body(grid_field, basis_values, support_lat, support_lon, lon_reach, mix_weights):
    lat_rows, half_lon, channels = grid_field.shape
    bands = lax.axis_size("lat")
    own = lax.axis_index("lon").astype(jnp.int32)
    both = ("lat", "lon")
    last = lat_rows - 1

    swapped = lax.ppermute(grid_field, "lon", [(0, 1), (1, 0)])
    up = range(bands - 1)
    same = [(2 * b, 2 * b + 2) for b in up] + [(2 * b + 3, 2 * b + 1) for b in up]
    cross = [(2 * b + 1, 2 * b + 2) for b in up] + [(2 * b + 2, 2 * b + 1) for b in up]
    ends = (grid_field[last:], grid_field[:1])
    beside_1 = lax.ppermute(jnp.where(own == 0, *ends), both, same)
    beside_2 = lax.ppermute(jnp.where(own == 1, *ends), both, cross)

    mix = mix_weights.reshape(K * channels, channels)
    even, odd = (jnp.asarray(t) for t in twiddles(2 * half_lon, bands))
    own_1 = own.reshape(1)

    support = (support_lat, support_lon, lon_reach)
    basis = jnp.transpose(basis_values, (0, 2, 1))
    rest = (support, own_1, basis, mix, even, odd)
    two = [grid_field, swapped]
    lone = circle_rows(1, *rest, two)
    moved_1 = lax.all_to_all(lone.reshape(2 * bands, 40, 128), both, 0, 0, tiled=True)
    pair = circle_rows(2, *rest, [*two, beside_1, beside_2])
    moved_2 = lax.all_to_all(pair.reshape(2 * bands, 80, 128), both, 0, 0, tiled=True)
    return gather(moved_1, moved_2).reshape(2, MMAX // bands, bands * lat_rows, channels // 2)


def solution(mesh):
    return jax.shard_map(
        body,
        mesh=mesh,
        in_specs=(
            P("lat", "lon", None),
            P("lat", None, None),
            P("lat", None),
            P("lat", None),
            P("lat"),
            P(),
        ),
        out_specs=P(None, "lat", None, "lon"),
        check_vma=False,
    )
```

```python
import functools

import jax
import jax.numpy as jnp
import ml_dtypes
import numpy as np
from jax import lax
from jax.experimental import pallas as pl
from jax.experimental.pallas import tpu as pltpu
from jax.sharding import PartitionSpec as P

MMAX = 640
K = 4
RLAT = 1
HMAX = 12
EDGE = 16
COLS = 48
SPAN = COLS + 2 * EDGE
DEPTH = 256
PITCH = 49
VMEM = 62 * 1024 * 1024


def exact_gelu(x):
    return 0.5 * x * (1.0 + lax.erf(x * 0.7071067811865476))


def row_kernel(outer, lat_ref, lon_ref, reach_ref, own_ref, basis_ref, *refs):
    mix_hbm, even_hbm, odd_hbm = refs[:3]
    n_in = 3 + 2 + 2 * outer
    ins, out_hbm, scratch = refs[3:n_in], refs[n_in], refs[n_in + 1 :]
    ext, agg, band, first, added, taken, left, out, mix_ref, even_ref, odd_ref = scratch[:11]
    row_sems, own_sems, out_sems = scratch[11:]
    own = own_ref[0]
    support = lat_ref.shape[1]
    half_lon = ins[0].shape[1]
    total_lon = 2 * half_lon
    channels = ext.shape[2]
    rows = ext.shape[0] - 2
    groups = out.shape[0]

    near_pieces = ((0, 0, half_lon), (1, 0, EDGE), (1, half_lon - EDGE, EDGE))
    pieces = (*near_pieces, (1, EDGE, half_lon - 2 * EDGE))

    def copy_of(n, p, core):
        side, begin, size = pieces[p]
        (ref, row), at_row = sources[n][side != core], sources[n][2]
        to = ext.at[at_row, pl.ds(EDGE + side * half_lon + begin, size)]
        return pltpu.make_async_copy(ref.at[row, pl.ds(begin, size)], to, row_sems.at[n, p])

    def start(n, p):
        for core in (0, 1):
            @pl.when(own == core)
            def _(core=core):
                copy_of(n, p, core).start()

    def wait(n, p):
        copy_of(n, p, 0).wait()

    field, swapped = ins[0], ins[1]
    if outer:
        sources = [((field, 3 * own + n), (swapped, 3 * own + n), 1 - own + n) for n in range(3)]
        sources.append(((ins[2], 0), (ins[3], 0), 3 * own))
        bases = [1 - own + step * (2 * own - 1) for step in range(rows)]
        lats = [4 * own + base for base in bases]
    else:
        sources = [((field, 1 + own + n), (swapped, 1 + own + n), n) for n in range(3)]
        bases, lats = [0], [2 + own]
    mix_copy = pltpu.make_async_copy(mix_hbm, mix_ref, own_sems.at[0])
    table_copies = (
        pltpu.make_async_copy(even_hbm, even_ref, own_sems.at[1]),
        pltpu.make_async_copy(odd_hbm, odd_ref, own_sems.at[2]),
    )
    for n in range(3):
        for p in range(3):
            start(n, p)
    mix_copy.start()
    for n in range(3):
        start(n, 3)
    for copy in table_copies:
        copy.start()
    for n in range(3, rows + 2):
        for p in range(4):
            start(n, p)

    pad = added.shape[0] - half_lon
    added[pl.ds(half_lon, pad), :] = jnp.zeros((pad, channels), added.dtype)
    taken[pl.ds(half_lon, pad), :] = jnp.zeros((pad, channels), added.dtype)
    sends = []

    def send(side, begin, size, n):
        copy = pltpu.make_async_copy(
            out.at[:, side, pl.ds(begin, size)],
            out_hbm.at[:, side, pl.ds(begin, size)],
            out_sems.at[n, side],
        )
        copy.start()
        sends.append(copy)

    lanes = lax.broadcasted_iota(jnp.int32, (support, DEPTH), 1)
    points = lax.broadcasted_iota(jnp.int32, (support, DEPTH), 0)
    width = channels // 2
    rest_size = 8 * rows
    for step in range(rows):
        here, base = lats[step], bases[step]
        reach = reach_ref[here]
        index = jnp.zeros((support, DEPTH), jnp.int32)
        for s in range(support):
            shift = jnp.minimum(jnp.maximum(lon_ref[here, s], -reach), reach)
            lane = (lat_ref[here, s] + RLAT) * SPAN + EDGE + shift
            index = jnp.where(points == s, lane, index)
        hits = jnp.where(lanes == index, 1.0, 0.0).astype(jnp.bfloat16)
        filters = jnp.dot(basis_ref[here], hits, preferred_element_type=jnp.float32)
        for k in range(K):
            same = jnp.broadcast_to(filters[k : k + 1], (8, DEPTH))
            for q in range(0, COLS, 16):
                pair = [pltpu.roll(same, q + e, 1, stride=1, stride_axis=0) for e in (0, 8)]
                band[pl.ds(k * COLS + q, 16), :] = jnp.concatenate(pair, axis=0).astype(band.dtype)

        fresh = range(0, 3) if step == 0 else range(step + 2, step + 3)
        for half in (0, 1):
            for n in fresh:
                for p in (range(3) if half == 0 else (3,)):
                    wait(n, p)
            if half == 0:
                for e in (sources[n][2] for n in fresh):
                    ext[e, pl.ds(0, EDGE), :] = ext[e, pl.ds(total_lon, EDGE), :]
                    ext[e, pl.ds(EDGE + total_lon, EDGE), :] = ext[e, pl.ds(EDGE, EDGE), :]
            for begin in range(half * half_lon, (half + 1) * half_lon, COLS):
                window = jnp.concatenate(
                    [ext[base + r, pl.ds(begin, SPAN), :] for r in range(3)]
                    + [ext[base, pl.ds(begin, DEPTH - 3 * SPAN), :]],
                    axis=0,
                )
                got = jnp.dot(band[...], window, preferred_element_type=jnp.float32).astype(agg.dtype)
                for k in range(K):
                    to = pl.ds(begin - half * half_lon, COLS), pl.ds(k * channels, channels)
                    agg[half, *to] = got[k * COLS : (k + 1) * COLS]
            if step == 0 and half == 0:
                mix_copy.wait()
            for n in range(0, channels, width):
                at_n = pl.ds(n, width)
                active = exact_gelu(
                    jnp.dot(agg[half], mix_ref[:, at_n], preferred_element_type=jnp.float32)
                )
                if half == 0:
                    first[:, at_n] = active
                else:
                    added[pl.ds(0, half_lon), at_n] = (first[:, at_n] + active).astype(added.dtype)
                    taken[pl.ds(0, half_lon), at_n] = (first[:, at_n] - active).astype(taken.dtype)

        if step == 0:
            for copy in table_copies:
                copy.wait()
        for side in (0, 1):
            at_n = pl.ds(side * width, width)
            even = jnp.dot(even_ref[...], added[:, at_n], preferred_element_type=jnp.float32)
            odd = jnp.dot(odd_ref[...], taken[:, at_n], preferred_element_type=jnp.float32)
            main = jnp.concatenate(
                [got[: groups * 8].reshape(groups, 8, width) for got in (even, odd)], axis=1
            ).astype(out.dtype)
            for h in (0, 1):
                c = 2 * step + h
                out[:, side, pl.ds(16 * c, 16), :] = main[:, :, h * 128 : (h + 1) * 128]
                for parity, got in ((0, even), (1, odd)):
                    for e in (0, 1):
                        where = pl.ds(4 * c + 2 * e + parity, groups, stride=rest_size)
                        rest = got[groups * (8 + e) : groups * (9 + e), h * 128 : (h + 1) * 128]
                        left[side, where, :] = rest
            send(side, 32 * step, 32, step)
            if step == rows - 1:
                rest = left[side].reshape(groups, rest_size, 128)
                out[:, side, pl.ds(32 * rows, rest_size), :] = rest.astype(out.dtype)
                send(side, 32 * rows, rest_size, rows)
    for copy in sends:
        copy.wait()


def circle_rows(rows, support, own, basis, mix, even, odd, arrays):
    _, half_lon, channels = arrays[0].shape
    groups = MMAX // 10
    smem = pl.BlockSpec(memory_space=pltpu.SMEM)
    hbm = pl.BlockSpec(memory_space=pl.ANY)
    wire = jax.ShapeDtypeStruct((groups, 2, 40 * rows, 128), jnp.bfloat16)
    return pl.pallas_call(
        functools.partial(row_kernel, int(len(arrays) > 2)),
        in_specs=[smem] * 4 + [pl.BlockSpec(memory_space=pltpu.VMEM)] + [hbm] * (3 + len(arrays)),
        out_specs=hbm,
        out_shape=wire,
        scratch_shapes=[
            pltpu.VMEM((rows + 2, 2 * half_lon + 2 * EDGE, channels), jnp.bfloat16),
            pltpu.VMEM((2, half_lon, K * channels), jnp.bfloat16),
            pltpu.VMEM((K * COLS, DEPTH), jnp.bfloat16),
            pltpu.VMEM((half_lon, channels), jnp.float32),
            pltpu.VMEM((even.shape[1], channels), jnp.bfloat16),
            pltpu.VMEM((even.shape[1], channels), jnp.bfloat16),
            pltpu.VMEM((2, groups * 8 * rows, 128), jnp.float32),
            pltpu.VMEM((groups, 2, 40 * rows, 128), jnp.bfloat16),
            pltpu.VMEM(mix.shape, jnp.bfloat16),
            pltpu.VMEM(even.shape, jnp.bfloat16),
            pltpu.VMEM(odd.shape, jnp.bfloat16),
            pltpu.SemaphoreType.DMA((rows + 2, 4)),
            pltpu.SemaphoreType.DMA((3,)),
            pltpu.SemaphoreType.DMA((rows + 1, 2)),
        ],
        compiler_params=pltpu.CompilerParams(vmem_limit_bytes=VMEM + (rows - 1) * 2**20),
        cost_estimate=pl.CostEstimate(
            flops=rows * (4 * half_lon * channels * (K * channels + 1024) + 4 * MMAX * half_lon * channels),
            bytes_accessed=4 * (rows + 2) * half_lon * channels + 2 * mix.size + 4 * even.size,
            transcendentals=0,
        ),
        name="circle_rows",
    )(*support, own, basis, mix, even, odd, *arrays)


def twiddles(total_lon, groups):
    half = total_lon // 2
    per = MMAX // groups
    cols = np.arange(half, dtype=np.int64)
    g = np.arange(groups)
    tables = []
    for parity in (0, 1):
        pairs = [(n, q) for n in g for q in range(8)] + [(n, q) for q in (8, 9) for n in g]
        group, place = np.array(pairs).T
        place = 2 * place + parity
        part, mode = place // per, group * per + place % per
        turn = (mode[:, None] * cols) % total_lon
        angles = turn.astype(np.float32) * np.float32(2.0 * np.pi / total_lon)
        scale = np.float32(1.0) / np.sqrt(np.float32(total_lon))
        table = np.zeros((MMAX, -(-half // 256) * 256), np.float32)
        table[:, :half] = np.where(part[:, None] == 0, np.cos(angles), -np.sin(angles)) * scale
        tables.append(table.astype(ml_dtypes.bfloat16))
    return tables


def gather_kernel(in_1, in_2, out_hbm, held_1, held_2, laid_0, laid_1, out, in_sems, out_sems):
    batches, sources, _, _ = held_1.shape
    modes, rows = out.shape[1:3]
    per = rows // sources
    laid = (laid_0, laid_1)

    def fetch(b, n):
        ref, held = ((in_1, held_1), (in_2, held_2))[n]
        return pltpu.make_async_copy(ref.at[pl.ds(b * sources, sources)], held.at[b], in_sems.at[b, n])

    def place(b):
        return pltpu.make_async_copy(out.at[b], out_hbm.at[:, pl.ds(b * rows, rows)], out_sems.at[b])

    def start(b, carry):
        for n in (0, 1):
            fetch(b, n).start()
        return carry

    lax.fori_loop(0, batches, start, 0)

    def one(b, carry):
        for n in (0, 1):
            fetch(b, n).wait()
        for g in range(sources):
            blocks = [held[b, g].astype(jnp.float32) for held in (held_1, held_2)]
            for step in range(per):
                lat = step if g % 2 else per - 1 - step
                for h in (0, 1):
                    if step == 0:
                        block, main, rest = blocks[0], 16 * h, 32 + 4 * h
                    else:
                        c = 2 * (step - 1) + h
                        block, main, rest = blocks[1], 16 * c, 64 + 4 * c
                    to = g * per + lat
                    laid[h][pl.ds(to, 8, stride=PITCH), :] = block[main : main + 8]
                    laid[h][pl.ds(8 * PITCH + to, 8, stride=PITCH), :] = block[main + 8 : main + 16]
                    laid[h][pl.ds(16 * PITCH + to, 4, stride=PITCH), :] = block[rest : rest + 4]
        for m in range(modes):
            slot = 8 * (m % 2) + m // 2 if m < 16 else m
            for h in (0, 1):
                piece = laid[h][pl.ds(slot * PITCH, rows), :]
                out[b, m, :, pl.ds(128 * h, 128)] = piece.astype(out.dtype)
        place(b).start()
        return carry

    lax.fori_loop(0, batches, one, 0)

    def end(b, carry):
        place(b).wait()
        return carry

    lax.fori_loop(0, batches, end, 0)


def gather(moved_1, moved_2):
    total, size, width = moved_1.shape
    sources = 16
    batches = total // sources
    modes = size // 2
    hbm = pl.BlockSpec(memory_space=pl.ANY)
    return pl.pallas_call(
        gather_kernel,
        in_specs=[hbm, hbm],
        out_specs=hbm,
        out_shape=jax.ShapeDtypeStruct((modes, total * 3, 2 * width), moved_1.dtype),
        scratch_shapes=[
            pltpu.VMEM((batches, sources, size, width), moved_1.dtype),
            pltpu.VMEM((batches, sources, 2 * size, width), moved_1.dtype),
            pltpu.VMEM((modes * PITCH, 128), jnp.float32),
            pltpu.VMEM((modes * PITCH, 128), jnp.float32),
            pltpu.VMEM((batches, modes, sources * 3, 2 * width), moved_1.dtype),
            pltpu.SemaphoreType.DMA((batches, 2)),
            pltpu.SemaphoreType.DMA((batches,)),
        ],
        compiler_params=pltpu.CompilerParams(vmem_limit_bytes=VMEM),
        name="gather",
    )(moved_1, moved_2)


def body(grid_field, basis_values, support_lat, support_lon, lon_reach, mix_weights):
    lat_rows, half_lon, channels = grid_field.shape
    bands = lax.axis_size("lat")
    own = lax.axis_index("lon").astype(jnp.int32)
    both = ("lat", "lon")
    last = lat_rows - 1

    swapped = lax.ppermute(grid_field, "lon", [(0, 1), (1, 0)])
    up = range(bands - 1)
    same = [(2 * b, 2 * b + 2) for b in up] + [(2 * b + 3, 2 * b + 1) for b in up]
    cross = [(2 * b + 1, 2 * b + 2) for b in up] + [(2 * b + 2, 2 * b + 1) for b in up]
    ends = (grid_field[last:], grid_field[:1])
    beside_1 = lax.ppermute(jnp.where(own == 0, *ends), both, same)
    beside_2 = lax.ppermute(jnp.where(own == 1, *ends), both, cross)

    mix = mix_weights.reshape(K * channels, channels)
    even, odd = (jnp.asarray(t) for t in twiddles(2 * half_lon, bands))
    own_1 = own.reshape(1)

    support = (support_lat, support_lon, lon_reach)
    basis = jnp.transpose(basis_values, (0, 2, 1))
    rest = (support, own_1, basis, mix, even, odd)
    two = [grid_field, swapped]
    lone = circle_rows(1, *rest, two)
    moved_1 = lax.all_to_all(lone.reshape(2 * bands, 40, 128), both, 0, 0, tiled=True)
    pair = circle_rows(2, *rest, [*two, beside_1, beside_2])
    moved_2 = lax.all_to_all(pair.reshape(2 * bands, 80, 128), both, 0, 0, tiled=True)
    return gather(moved_1, moved_2).reshape(2, MMAX // bands, bands * lat_rows, channels // 2)


def solution(mesh):
    return jax.shard_map(
        body,
        mesh=mesh,
        in_specs=(
            P("lat", "lon", None),
            P("lat", None, None),
            P("lat", None),
            P("lat", None),
            P("lat"),
            P(),
        ),
        out_specs=P(None, "lat", None, "lon"),
        check_vma=False,
    )
```

```python
import functools

import jax
import jax.numpy as jnp
import ml_dtypes
import numpy as np
from jax import lax
from jax.experimental import pallas as pl
from jax.experimental.pallas import tpu as pltpu
from jax.sharding import PartitionSpec as P

MMAX = 640
K = 4
RLAT = 1
HMAX = 12
EDGE = 16
COLS = 48
SPAN = COLS + 2 * EDGE
DEPTH = 256
PITCH = 49
VMEM = 62 * 1024 * 1024


def exact_gelu(x):
    return 0.5 * x * (1.0 + lax.erf(x * 0.7071067811865476))


def row_kernel(outer, lat_ref, lon_ref, reach_ref, own_ref, basis_ref, *refs):
    mix_hbm, even_hbm, odd_hbm = refs[:3]
    n_in = 3 + 2 + 2 * outer
    ins, out_hbm, scratch = refs[3:n_in], refs[n_in], refs[n_in + 1 :]
    ext, agg, band, first, added, taken, left, out, mix_ref, even_ref, odd_ref = scratch[:11]
    row_sems, own_sems, out_sems = scratch[11:]
    own = own_ref[0]
    support = lat_ref.shape[1]
    half_lon = ins[0].shape[1]
    total_lon = 2 * half_lon
    channels = ext.shape[2]
    rows = ext.shape[0] - 2
    groups = out.shape[0]

    near_pieces = ((0, 0, half_lon), (1, 0, EDGE), (1, half_lon - EDGE, EDGE))
    pieces = (*near_pieces, (1, EDGE, half_lon - 2 * EDGE))

    def copy_of(n, p, core):
        side, begin, size = pieces[p]
        (ref, row), at_row = sources[n][side != core], sources[n][2]
        to = ext.at[at_row, pl.ds(EDGE + side * half_lon + begin, size)]
        return pltpu.make_async_copy(ref.at[row, pl.ds(begin, size)], to, row_sems.at[n, p])

    def wait(n, p):
        copy_of(n, p, 0).wait()

    field, swapped = ins[0], ins[1]
    if outer:
        sources = [((field, 3 * own + n), (swapped, 3 * own + n), 1 - own + n) for n in range(3)]
        sources.append(((ins[2], 0), (ins[3], 0), 3 * own))
        bases = [1 - own + step * (2 * own - 1) for step in range(rows)]
        lats = [4 * own + base for base in bases]
    else:
        sources = [((field, 1 + own + n), (swapped, 1 + own + n), n) for n in range(3)]
        bases, lats = [0], [2 + own]
    mix_copy = pltpu.make_async_copy(mix_hbm, mix_ref, own_sems.at[0])
    table_copies = (
        pltpu.make_async_copy(even_hbm, even_ref, own_sems.at[1]),
        pltpu.make_async_copy(odd_hbm, odd_ref, own_sems.at[2]),
    )
    for core in (0, 1):
        @pl.when(own == core)
        def _(core=core):
            for n in range(3):
                for p in range(3):
                    copy_of(n, p, core).start()
            mix_copy.start()
            for n in range(3):
                copy_of(n, 3, core).start()
            for copy in table_copies:
                copy.start()
            for n in range(3, rows + 2):
                for p in range(4):
                    copy_of(n, p, core).start()

    pad = added.shape[0] - half_lon
    added[pl.ds(half_lon, pad), :] = jnp.zeros((pad, channels), added.dtype)
    taken[pl.ds(half_lon, pad), :] = jnp.zeros((pad, channels), added.dtype)
    sends = []

    def send(side, begin, size, n):
        copy = pltpu.make_async_copy(
            out.at[:, side, pl.ds(begin, size)],
            out_hbm.at[:, side, pl.ds(begin, size)],
            out_sems.at[n, side],
        )
        copy.start()
        sends.append(copy)

    lanes = lax.broadcasted_iota(jnp.int32, (support, DEPTH), 1)
    points = lax.broadcasted_iota(jnp.int32, (support, DEPTH), 0)
    width = channels // 2
    rest_size = 8 * rows
    for step in range(rows):
        here, base = lats[step], bases[step]
        reach = reach_ref[here]
        index = jnp.zeros((support, DEPTH), jnp.int32)
        for s in range(support):
            shift = jnp.minimum(jnp.maximum(lon_ref[here, s], -reach), reach)
            lane = (lat_ref[here, s] + RLAT) * SPAN + EDGE + shift
            index = jnp.where(points == s, lane, index)
        hits = jnp.where(lanes == index, 1.0, 0.0).astype(jnp.bfloat16)
        filters = jnp.dot(basis_ref[here], hits, preferred_element_type=jnp.float32)
        for k in range(K):
            same = jnp.broadcast_to(filters[k : k + 1], (8, DEPTH))
            for q in range(0, COLS, 16):
                pair = [pltpu.roll(same, q + e, 1, stride=1, stride_axis=0) for e in (0, 8)]
                band[pl.ds(k * COLS + q, 16), :] = jnp.concatenate(pair, axis=0).astype(band.dtype)

        fresh = range(0, 3) if step == 0 else range(step + 2, step + 3)
        for half in (0, 1):
            for n in fresh:
                for p in (range(3) if half == 0 else (3,)):
                    wait(n, p)
            if half == 0:
                for e in (sources[n][2] for n in fresh):
                    ext[e, pl.ds(0, EDGE), :] = ext[e, pl.ds(total_lon, EDGE), :]
                    ext[e, pl.ds(EDGE + total_lon, EDGE), :] = ext[e, pl.ds(EDGE, EDGE), :]
            for begin in range(half * half_lon, (half + 1) * half_lon, COLS):
                window = jnp.concatenate(
                    [ext[base + r, pl.ds(begin, SPAN), :] for r in range(3)]
                    + [ext[base, pl.ds(begin, DEPTH - 3 * SPAN), :]],
                    axis=0,
                )
                got = jnp.dot(band[...], window, preferred_element_type=jnp.float32).astype(agg.dtype)
                for k in range(K):
                    to = pl.ds(begin - half * half_lon, COLS), pl.ds(k * channels, channels)
                    agg[half, *to] = got[k * COLS : (k + 1) * COLS]
            if step == 0 and half == 0:
                mix_copy.wait()
            for n in range(0, channels, width):
                at_n = pl.ds(n, width)
                active = exact_gelu(
                    jnp.dot(agg[half], mix_ref[:, at_n], preferred_element_type=jnp.float32)
                )
                if half == 0:
                    first[:, at_n] = active
                else:
                    added[pl.ds(0, half_lon), at_n] = (first[:, at_n] + active).astype(added.dtype)
                    taken[pl.ds(0, half_lon), at_n] = (first[:, at_n] - active).astype(taken.dtype)

        if step == 0:
            for copy in table_copies:
                copy.wait()
        for side in (0, 1):
            at_n = pl.ds(side * width, width)
            even = jnp.dot(even_ref[...], added[:, at_n], preferred_element_type=jnp.float32)
            odd = jnp.dot(odd_ref[...], taken[:, at_n], preferred_element_type=jnp.float32)
            main = jnp.concatenate(
                [got[: groups * 8].reshape(groups, 8, width) for got in (even, odd)], axis=1
            ).astype(out.dtype)
            for h in (0, 1):
                c = 2 * step + h
                out[:, side, pl.ds(16 * c, 16), :] = main[:, :, h * 128 : (h + 1) * 128]
                for parity, got in ((0, even), (1, odd)):
                    for e in (0, 1):
                        where = pl.ds(4 * c + 2 * e + parity, groups, stride=rest_size)
                        rest = got[groups * (8 + e) : groups * (9 + e), h * 128 : (h + 1) * 128]
                        left[side, where, :] = rest
            send(side, 32 * step, 32, step)
            if step == rows - 1:
                rest = left[side].reshape(groups, rest_size, 128)
                out[:, side, pl.ds(32 * rows, rest_size), :] = rest.astype(out.dtype)
                send(side, 32 * rows, rest_size, rows)
    for copy in sends:
        copy.wait()


def circle_rows(rows, support, own, basis, mix, even, odd, arrays):
    _, half_lon, channels = arrays[0].shape
    groups = MMAX // 10
    smem = pl.BlockSpec(memory_space=pltpu.SMEM)
    hbm = pl.BlockSpec(memory_space=pl.ANY)
    wire = jax.ShapeDtypeStruct((groups, 2, 40 * rows, 128), jnp.bfloat16)
    return pl.pallas_call(
        functools.partial(row_kernel, int(len(arrays) > 2)),
        in_specs=[smem] * 4 + [pl.BlockSpec(memory_space=pltpu.VMEM)] + [hbm] * (3 + len(arrays)),
        out_specs=hbm,
        out_shape=wire,
        scratch_shapes=[
            pltpu.VMEM((rows + 2, 2 * half_lon + 2 * EDGE, channels), jnp.bfloat16),
            pltpu.VMEM((2, half_lon, K * channels), jnp.bfloat16),
            pltpu.VMEM((K * COLS, DEPTH), jnp.bfloat16),
            pltpu.VMEM((half_lon, channels), jnp.float32),
            pltpu.VMEM((even.shape[1], channels), jnp.bfloat16),
            pltpu.VMEM((even.shape[1], channels), jnp.bfloat16),
            pltpu.VMEM((2, groups * 8 * rows, 128), jnp.float32),
            pltpu.VMEM((groups, 2, 40 * rows, 128), jnp.bfloat16),
            pltpu.VMEM(mix.shape, jnp.bfloat16),
            pltpu.VMEM(even.shape, jnp.bfloat16),
            pltpu.VMEM(odd.shape, jnp.bfloat16),
            pltpu.SemaphoreType.DMA((rows + 2, 4)),
            pltpu.SemaphoreType.DMA((3,)),
            pltpu.SemaphoreType.DMA((rows + 1, 2)),
        ],
        compiler_params=pltpu.CompilerParams(vmem_limit_bytes=VMEM + (rows - 1) * 2**20),
        cost_estimate=pl.CostEstimate(
            flops=rows * (4 * half_lon * channels * (K * channels + 1024) + 4 * MMAX * half_lon * channels),
            bytes_accessed=4 * (rows + 2) * half_lon * channels + 2 * mix.size + 4 * even.size,
            transcendentals=0,
        ),
        name="circle_rows",
    )(*support, own, basis, mix, even, odd, *arrays)


def twiddles(total_lon, groups):
    half = total_lon // 2
    per = MMAX // groups
    cols = np.arange(half, dtype=np.int64)
    g = np.arange(groups)
    tables = []
    for parity in (0, 1):
        pairs = [(n, q) for n in g for q in range(8)] + [(n, q) for q in (8, 9) for n in g]
        group, place = np.array(pairs).T
        place = 2 * place + parity
        part, mode = place // per, group * per + place % per
        turn = (mode[:, None] * cols) % total_lon
        angles = turn.astype(np.float32) * np.float32(2.0 * np.pi / total_lon)
        scale = np.float32(1.0) / np.sqrt(np.float32(total_lon))
        table = np.zeros((MMAX, -(-half // 256) * 256), np.float32)
        table[:, :half] = np.where(part[:, None] == 0, np.cos(angles), -np.sin(angles)) * scale
        tables.append(table.astype(ml_dtypes.bfloat16))
    return tables


def gather_kernel(in_1, in_2, out_hbm, held_1, held_2, laid_0, laid_1, out, in_sems, out_sems):
    batches, sources, _, _ = held_1.shape
    modes, rows = out.shape[1:3]
    per = rows // sources
    laid = (laid_0, laid_1)

    def fetch(b, n):
        ref, held = ((in_1, held_1), (in_2, held_2))[n]
        return pltpu.make_async_copy(ref.at[pl.ds(b * sources, sources)], held.at[b], in_sems.at[b, n])

    def place(b):
        return pltpu.make_async_copy(out.at[b], out_hbm.at[:, pl.ds(b * rows, rows)], out_sems.at[b])

    def start(b, carry):
        for n in (0, 1):
            fetch(b, n).start()
        return carry

    lax.fori_loop(0, batches, start, 0)

    def one(b, carry):
        for n in (0, 1):
            fetch(b, n).wait()
        for g in range(sources):
            blocks = [held[b, g].astype(jnp.float32) for held in (held_1, held_2)]
            for step in range(per):
                lat = step if g % 2 else per - 1 - step
                for h in (0, 1):
                    if step == 0:
                        block, main, rest = blocks[0], 16 * h, 32 + 4 * h
                    else:
                        c = 2 * (step - 1) + h
                        block, main, rest = blocks[1], 16 * c, 64 + 4 * c
                    to = g * per + lat
                    laid[h][pl.ds(to, 8, stride=PITCH), :] = block[main : main + 8]
                    laid[h][pl.ds(8 * PITCH + to, 8, stride=PITCH), :] = block[main + 8 : main + 16]
                    laid[h][pl.ds(16 * PITCH + to, 4, stride=PITCH), :] = block[rest : rest + 4]
        for m in range(modes):
            slot = 8 * (m % 2) + m // 2 if m < 16 else m
            for h in (0, 1):
                piece = laid[h][pl.ds(slot * PITCH, rows), :]
                out[b, m, :, pl.ds(128 * h, 128)] = piece.astype(out.dtype)
        place(b).start()
        return carry

    lax.fori_loop(0, batches, one, 0)

    def end(b, carry):
        place(b).wait()
        return carry

    lax.fori_loop(0, batches, end, 0)


def gather(moved_1, moved_2):
    total, size, width = moved_1.shape
    sources = 16
    batches = total // sources
    modes = size // 2
    hbm = pl.BlockSpec(memory_space=pl.ANY)
    return pl.pallas_call(
        gather_kernel,
        in_specs=[hbm, hbm],
        out_specs=hbm,
        out_shape=jax.ShapeDtypeStruct((modes, total * 3, 2 * width), moved_1.dtype),
        scratch_shapes=[
            pltpu.VMEM((batches, sources, size, width), moved_1.dtype),
            pltpu.VMEM((batches, sources, 2 * size, width), moved_1.dtype),
            pltpu.VMEM((modes * PITCH, 128), jnp.float32),
            pltpu.VMEM((modes * PITCH, 128), jnp.float32),
            pltpu.VMEM((batches, modes, sources * 3, 2 * width), moved_1.dtype),
            pltpu.SemaphoreType.DMA((batches, 2)),
            pltpu.SemaphoreType.DMA((batches,)),
        ],
        compiler_params=pltpu.CompilerParams(vmem_limit_bytes=VMEM),
        name="gather",
    )(moved_1, moved_2)


def body(grid_field, basis_values, support_lat, support_lon, lon_reach, mix_weights):
    lat_rows, half_lon, channels = grid_field.shape
    bands = lax.axis_size("lat")
    own = lax.axis_index("lon").astype(jnp.int32)
    both = ("lat", "lon")
    last = lat_rows - 1

    swapped = lax.ppermute(grid_field, "lon", [(0, 1), (1, 0)])
    up = range(bands - 1)
    same = [(2 * b, 2 * b + 2) for b in up] + [(2 * b + 3, 2 * b + 1) for b in up]
    cross = [(2 * b + 1, 2 * b + 2) for b in up] + [(2 * b + 2, 2 * b + 1) for b in up]
    ends = (grid_field[last:], grid_field[:1])
    beside_1 = lax.ppermute(jnp.where(own == 0, *ends), both, same)
    beside_2 = lax.ppermute(jnp.where(own == 1, *ends), both, cross)

    mix = mix_weights.reshape(K * channels, channels)
    even, odd = (jnp.asarray(t) for t in twiddles(2 * half_lon, bands))
    own_1 = own.reshape(1)

    support = (support_lat, support_lon, lon_reach)
    basis = jnp.transpose(basis_values, (0, 2, 1))
    rest = (support, own_1, basis, mix, even, odd)
    two = [grid_field, swapped]
    lone = circle_rows(1, *rest, two)
    moved_1 = lax.all_to_all(lone.reshape(2 * bands, 40, 128), both, 0, 0, tiled=True)
    pair = circle_rows(2, *rest, [*two, beside_1, beside_2])
    moved_2 = lax.all_to_all(pair.reshape(2 * bands, 80, 128), both, 0, 0, tiled=True)
    return gather(moved_1, moved_2).reshape(2, MMAX // bands, bands * lat_rows, channels // 2)


def solution(mesh):
    return jax.shard_map(
        body,
        mesh=mesh,
        in_specs=(
            P("lat", "lon", None),
            P("lat", None, None),
            P("lat", None),
            P("lat", None),
            P("lat"),
            P(),
        ),
        out_specs=P(None, "lat", None, "lon"),
        check_vma=False,
    )
```
